32 devices in a mesh: dp: 8 (over z, y), order: 4 (over x, core).
Axes of the slice: x: 2, y: 2, z: 4, core: 2. Of those that a mesh axis runs over, the one named last changes fastest.
Arguments:
- images: bfloat16 [1024, 128, 512], P(('dp', 'order')), may hold values from -6 to 6
- radial_interp: bfloat16 [128, 128], replicated, may hold values from -0.5 to 0.5
- assignment: int32 [256], replicated, may hold values from 0 to 255, as said below
- counts: int32 [256], P('order'), may hold values from 32 to 128, as said below
- radial_basis: bfloat16 [256, 128, 128], P('order'), may hold values from -0.5 to 0.5
- eigenbasis: bfloat16 [256, 128, 128], P('order'), may hold values from -0.5 to 0.5
Outputs:
- covariance: float32 [256, 32768], P(('order', 'dp'))
- projected: bfloat16 [2, 256, 1024, 128], P(None, 'order', 'dp')
The draws below stay inside these ranges and needn't reach their ends.
Inputs may be any that keep to these rules, and one draw needn't show every extreme that they name: `assignment`: a permutation of the orders 0 to 255. The slot of order 0 keeps 128; the slot of order 256 - 1 keeps 32; counts fall with the order up to a jitter of 3.
All inputs are finite; a program needn't handle non-finite values.
Results may differ from the reference program's by a relative error of at most 0.013.
Values may be sent and summed in bfloat16 or wider, within the bound.
A program may use at most 128 MiB of HBM per device.

```python
import math
import jax
import jax.numpy as jnp
from jax import lax

NA = 512
NR0 = 128
NR = 128
NK = 128
NE = 128
IMG_DEV = 32
ORDERS = 256
NK_MIN = 32
IMAGES = 1024
N_ORDER = 4


def shared_order(key):
    return jax.random.permutation(jax.random.fold_in(key, 7), ORDERS).astype(jnp.int32)


def draw_assignment(key, part):
    return shared_order(key)


def draw_counts(key, part):
    order_ids = shared_order(key)
    jitter = jax.random.randint(jax.random.fold_in(key, 11), (ORDERS,), 0, 4).astype(jnp.int32)
    jitter = jnp.where(order_ids == 0, 0, jitter)
    base_count = NK - (NK - NK_MIN) * order_ids // (ORDERS - 1)
    return jnp.maximum(NK_MIN, base_count - jitter).astype(jnp.int32)


def block_levels(stream_key, dims, split, low, top_value):
    gain, own = 1.0, jax.random.fold_in(stream_key, 6)
    for axis_at, blocks in split:
        heights = jnp.exp(jax.random.uniform(jax.random.fold_in(own, axis_at), (blocks,), jnp.float32, low / len(split), top_value / len(split)))
        gain = gain * jnp.repeat(heights, dims[axis_at] // blocks).reshape([-1 if axis == axis_at else 1 for axis in range(len(dims))])
    return gain


def noise(own_key, extent, scale, bound, shards=(), held_as=jnp.bfloat16):
    level = block_levels(own_key, extent, shards, -0.22, 0.18) if shards else 1.0
    values = jax.random.normal(own_key, extent, jnp.float32) * scale * level
    return jnp.minimum(jnp.maximum(values, -bound), bound).astype(held_as)


def setup_inputs(seed: int = 0) -> dict:
    arg_keys = jax.random.split(jax.random.key(seed), 7)
    return {
        "images": noise(arg_keys[0], (IMAGES, NR0, NA), 1.0, 6.0, ((0, 32),)),
        "radial_interp": noise(arg_keys[1], (NR0, NR), NR0 ** -0.5, 0.5),
        "assignment": draw_assignment(jax.random.fold_in(arg_keys[6], 71), 0),
        "counts": draw_counts(jax.random.fold_in(arg_keys[6], 71), 0),
        "radial_basis": noise(arg_keys[4], (ORDERS, NR, NK), NR ** -0.5, 0.5, ((0, 4),)),
        "eigenbasis": noise(arg_keys[5], (ORDERS, NK, NE), NK ** -0.5, 0.5, ((0, 4),)),
    }


def build_table(slot_orders, samples):
    angle_index = jnp.arange(samples, dtype=jnp.int32)[:, None]
    product = angle_index * slot_orders[None, :].astype(jnp.int32) % samples
    theta = product.astype(jnp.float32) * (2.0 * math.pi / samples)
    factor = 1.0 / math.sqrt(samples)
    return (jnp.concatenate([jnp.cos(theta), -jnp.sin(theta)], axis=1) * factor).astype(jnp.bfloat16)

def reference(images, radial_interp, assignment, counts, radial_basis, eigenbasis):
    dft_table = build_table(assignment, NA).astype(jnp.float32)
    kept_mask = (jnp.arange(NK, dtype=jnp.int32)[None, :] < counts[:, None]).astype(jnp.bfloat16)
    kept_basis = (radial_basis * kept_mask[:, None, :]).astype(jnp.float32)
    interp_wide = radial_interp.astype(jnp.float32)
    eigen_wide = eigenbasis.astype(jnp.float32)
    block_size = IMG_DEV * N_ORDER
    blocks = images.reshape(IMAGES // block_size, block_size, NR0, NA)

    def one_block(carry, block_images):
        polar_grid = jnp.einsum('isa,sr->ira', block_images.astype(jnp.float32), interp_wide).astype(jnp.bfloat16)
        spectrum = jnp.einsum('ira,ac->cir', polar_grid.astype(jnp.float32), dft_table).astype(jnp.bfloat16)
        spectrum = spectrum.reshape(2, ORDERS, block_size, NR).astype(jnp.float32)
        coefficients = jnp.einsum('pkir,krj->pkij', spectrum, kept_basis).astype(jnp.bfloat16).astype(jnp.float32)
        real_cov = jnp.einsum('pkij,pkil->kjl', coefficients, coefficients)
        imag_cov = jnp.einsum('kij,kil->kjl', coefficients[1], coefficients[0]) - jnp.einsum('kij,kil->kjl', coefficients[0], coefficients[1])
        projected_block = jnp.einsum('pkij,kje->pkie', coefficients, eigen_wide).astype(jnp.bfloat16)
        return (carry + jnp.stack([real_cov, imag_cov], 0), projected_block)
    start_cov = jnp.zeros((2, ORDERS, NK, NK), jnp.float32)
    summed_cov, projected_all = lax.scan(one_block, start_cov, blocks)
    projected = projected_all.transpose(1, 2, 0, 3, 4).reshape(2, ORDERS, IMAGES, NE)
    covariance = (summed_cov / IMAGES).transpose(1, 0, 2, 3).reshape(ORDERS, 2 * NK * NK)
    return (covariance, projected)
```

```python
import math

import jax
import jax.numpy as jnp
from jax import lax
from jax.sharding import PartitionSpec as P


def build_table(slot_orders, samples):
    angle_index = jnp.arange(samples, dtype=jnp.int32)[:, None]
    product = angle_index * slot_orders[None, :] % samples
    theta = product.astype(jnp.float32) * (2.0 * math.pi / samples)
    factor = 1.0 / math.sqrt(samples)
    return (jnp.concatenate([jnp.cos(theta), -jnp.sin(theta)], axis=1) * factor).astype(
        jnp.bfloat16
    )


def body(images, radial_interp, assignment, counts, radial_basis, eigenbasis):
    local_images = images.shape[0]
    samples = images.shape[2]
    nodes = radial_interp.shape[1]
    slot_total = assignment.shape[0]
    basis_width = radial_basis.shape[2]
    dft_table = build_table(assignment, samples)
    spectrum = jnp.einsum(
        "isa,ac->cis", images, dft_table, preferred_element_type=jnp.float32
    ).astype(jnp.bfloat16)
    spectrum = spectrum.reshape(2, slot_total, local_images, nodes)
    owned_spec = lax.all_to_all(spectrum, "order", split_axis=1, concat_axis=2, tiled=True)
    kept_mask = (jnp.arange(basis_width, dtype=jnp.int32)[None, :] < counts[:, None]).astype(
        jnp.bfloat16
    )
    kept_basis = jnp.einsum(
        "sr,krj->ksj",
        radial_interp,
        radial_basis * kept_mask[:, None, :],
        preferred_element_type=jnp.float32,
    ).astype(jnp.bfloat16)
    coefficients = jnp.einsum(
        "pkir,krj->pkij", owned_spec, kept_basis, preferred_element_type=jnp.float32
    ).astype(jnp.bfloat16)
    mixed = jnp.stack(
        [coefficients[0] - coefficients[1], coefficients[0] + coefficients[1]], 0
    )
    image_total = coefficients.shape[2] * lax.axis_size("dp")
    partial_cov = (
        jnp.einsum("pkij,pkil->kjl", coefficients, mixed, preferred_element_type=jnp.float32)
        / image_total
    )
    summed = lax.psum_scatter(
        partial_cov.astype(jnp.bfloat16), "dp", scatter_dimension=0, tiled=True
    ).astype(jnp.float32)
    flipped = summed.transpose(0, 2, 1)
    covariance = jnp.stack([summed + flipped, summed - flipped], 1) * 0.5
    covariance = covariance.reshape(summed.shape[0], 2 * basis_width * basis_width)
    projected = jnp.einsum(
        "pkij,kje->pkie", coefficients, eigenbasis, preferred_element_type=jnp.float32
    ).astype(jnp.bfloat16)
    return (covariance, projected)


def solution(mesh):
    placed = (
        P(("dp", "order"), None, None),
        P(),
        P(),
        P("order"),
        P("order", None, None),
        P("order", None, None),
    )
    return jax.shard_map(
        body,
        mesh=mesh,
        in_specs=placed,
        out_specs=(P(("order", "dp"), None), P(None, "order", "dp", None)),
        check_vma=False,
    )
```

```python
import functools
import math

import jax
import jax.numpy as jnp
import ml_dtypes
import numpy as np
from jax import lax
from jax.experimental import pallas as pl
from jax.experimental.pallas import tpu as pltpu
from jax.sharding import PartitionSpec as P

MESH = pl.DeviceIdType.MESH
BF16 = jnp.bfloat16
F32 = jnp.float32
CORES = 2
WINDOW = 4


def base_table(orders, samples):
    angle = (np.arange(orders)[:, None] * np.arange(samples)[None, :]) % samples
    theta = angle.astype(np.float32) * np.float32(2.0 * math.pi / samples)
    rows = np.concatenate([np.cos(theta), -np.sin(theta)], 0) / np.sqrt(np.float32(samples))
    return rows.astype(ml_dtypes.bfloat16)


def kernel(
    n_order, n_dp, images_hbm, interp, row_index, base, mask, basis_hbm, eigen_hbm,
    cov_out, proj_out,
    images, basis, eigen, table, kept, wide, send, recv, proj, cov_own, cov_y, cov_z, cov_got,
    cov_rows, image_sem, weight_sem, spec_send, spec_recv, y_send, y_recv, z_send, z_recv, proj_sem,
):
    local_images, nodes, samples = images.shape
    slots = basis.shape[0]
    chips, half, per_dp = n_order // CORES, n_dp // 2, slots // n_dp
    chip_rows = CORES * slots * 2
    block = 2 * n_dp * local_images
    me, my_dp = lax.axis_index("order"), lax.axis_index("dp")
    my_chip, my_core = me // CORES, me % CORES
    my_z, my_y = my_dp // 2, my_dp % 2

    def order_of(dx, dc):
        return lax.rem(my_chip + dx, chips) * CORES + lax.rem(my_core + dc, CORES)

    peers = [(dx, dc) for dx in range(1, chips) for dc in range(CORES)] + [(0, 1)]
    y_peer = my_z * 2 + (1 - my_y)

    def z_peer(q):
        return lax.rem(my_z + q, half)

    barrier = pltpu.get_barrier_semaphore()
    for dx, dc in peers:
        pl.semaphore_signal(barrier, 1, device_id={"order": order_of(dx, dc)}, device_id_type=MESH)
    pl.semaphore_signal(barrier, 1, device_id={"dp": y_peer}, device_id_type=MESH)
    for q in range(1, half):
        pl.semaphore_signal(
            barrier, 1, device_id={"dp": z_peer(q) * 2 + my_y}, device_id_type=MESH
        )

    parts = image_sem.shape[0]
    per_part = local_images // parts
    image_copies = [
        pltpu.make_async_copy(
            images_hbm.at[pl.ds(n * per_part, per_part)],
            images.at[pl.ds(n * per_part, per_part)],
            image_sem.at[n],
        )
        for n in range(parts)
    ]
    for copy in image_copies:
        copy.start()
    basis_copy = pltpu.make_async_copy(basis_hbm, basis, weight_sem.at[0])
    eigen_copy = pltpu.make_async_copy(eigen_hbm, eigen, weight_sem.at[1])
    basis_copy.start()
    eigen_copy.start()

    total_rows = table.shape[0]
    for r in range(0, total_rows, 128):
        hot = row_index[pl.ds(r, 128), :] == lax.broadcasted_iota(
            jnp.int32, (128, base.shape[0]), 1
        )
        table[pl.ds(r, 128), :] = jnp.dot(
            hot.astype(F32).astype(BF16), base[...], preferred_element_type=F32
        ).astype(BF16)

    def transform(dx, first):
        start = pl.multiple_of(lax.rem(my_chip + dx, chips) * chip_rows, chip_rows)
        for n in range(parts):
            if first:
                image_copies[n].wait()

            @pl.loop(0, per_part // 2)
            def _(h):
                i = n * per_part + h * 2
                pair = images[pl.ds(i, 2)].reshape(2 * nodes, samples)
                got = lax.dot_general(
                    table[pl.ds(start, chip_rows), :], pair,
                    (((1,), (1,)), ((), ())), preferred_element_type=F32,
                )
                wide[pl.ds(i, chip_rows, stride=local_images), :] = got[:, :nodes]
                wide[pl.ds(i + 1, chip_rows, stride=local_images), :] = got[:, nodes:]

    def spec_copy(k, t):
        dx, dc = peers[t]
        return pltpu.make_async_remote_copy(
            src_ref=send.at[t, k],
            dst_ref=recv.at[k, me],
            send_sem=spec_send.at[t, k],
            recv_sem=spec_recv.at[t, k],
            device_id={"order": order_of(dx, dc)},
            device_id_type=MESH,
        )

    def rows_of(dc, k):
        return pl.ds(
            pl.multiple_of((lax.rem(my_core + dc, CORES) * per_dp + k) * block, block), block
        )

    far = len(peers) - 1
    for dx in range(1, chips):
        transform(dx, dx == 1)
        if dx == 1:
            pl.semaphore_wait(barrier, len(peers) + half)
        for k in range(per_dp):
            for dc in range(CORES):
                t = (dx - 1) * CORES + dc
                send[t, k] = wide[rows_of(dc, k), :].astype(BF16)
                if k < WINDOW:
                    spec_copy(k, t).start()
    transform(0, chips == 1)
    for k in range(per_dp):
        send[far, k] = wide[rows_of(1, k), :].astype(BF16)
        spec_copy(k, far).start()
    for k in range(per_dp):
        recv[k, me] = wide[rows_of(0, k), :].astype(BF16)

    basis_copy.wait()

    @pl.loop(0, slots)
    def _(j):
        kept[j] = (
            jnp.dot(interp[...], basis[j], preferred_element_type=F32) * mask[j]
        ).astype(BF16)

    eigen_copy.wait()
    scale = 1.0 / (local_images * n_order * n_dp)

    def y_copy(k):
        return pltpu.make_async_remote_copy(
            src_ref=cov_own.at[k, 1 - my_y],
            dst_ref=cov_y.at[k],
            send_sem=y_send.at[k],
            recv_sem=y_recv.at[k],
            device_id={"dp": y_peer},
            device_id_type=MESH,
        )

    def z_copy(k, q):
        return pltpu.make_async_remote_copy(
            src_ref=cov_z.at[k, z_peer(q)],
            dst_ref=cov_got.at[k, q],
            send_sem=z_send.at[k, q],
            recv_sem=z_recv.at[k, q],
            device_id={"dp": z_peer(q) * 2 + my_y},
            device_id_type=MESH,
        )

    def proj_copy(k):
        return pltpu.make_async_copy(proj.at[k], proj_out.at[:, :, k], proj_sem.at[k])

    def slot_work(k):
        @pl.loop(0, half)
        def _(z):
            for y in range(2):
                d = z * 2 + y
                j = d * per_dp + k
                at = pl.multiple_of(d * 2 * local_images, 2 * local_images)
                got = recv[k, :, pl.ds(at, 2 * local_images), :]
                both = jnp.concatenate(
                    [got[:, :local_images], got[:, local_images:]], 0
                ).reshape(2 * n_order * local_images, nodes)
                coef = jnp.dot(both, kept[j], preferred_element_type=F32).astype(BF16)
                real, imag = coef[: n_order * local_images], coef[n_order * local_images :]
                mixed = jnp.concatenate([real - imag, real + imag], 0)
                cov = lax.dot_general(
                    coef, mixed, (((0,), (0,)), ((), ())), preferred_element_type=F32
                )
                cov_own[k, y, z] = (cov * scale).astype(BF16)
                out = jnp.dot(coef, eigen[j], preferred_element_type=F32).astype(BF16)
                proj[k, 0, d] = out[: n_order * local_images]
                proj[k, 1, d] = out[n_order * local_images :]

    def reduce_y(k):
        y_copy(k).wait_recv()
        cov_z[k] = (cov_own[k, my_y].astype(F32) + cov_y[k].astype(F32)).astype(BF16)
        for q in range(1, half):
            z_copy(k, q).start()

    def reduce_z(k):
        whole = cov_z[k, my_z].astype(F32)
        for q in range(1, half):
            z_copy(k, q).wait_recv()
            whole = whole + cov_got[k, q].astype(F32)
        flipped = whole.T
        width = whole.shape[0]
        cov_rows[pl.ds(k, width, stride=per_dp), :] = (whole + flipped) * 0.5
        cov_rows[pl.ds(width * per_dp + k, width, stride=per_dp), :] = (whole - flipped) * 0.5

    for k in range(per_dp):
        if k + WINDOW < per_dp:
            for t in range(far):
                spec_copy(k + WINDOW, t).start()
        for t in range(len(peers)):
            spec_copy(k, t).wait_recv()
        slot_work(k)
        y_copy(k).start()
        proj_copy(k).start()
        if k >= 1:
            reduce_y(k - 1)
        if k >= 2:
            reduce_z(k - 2)
    reduce_y(per_dp - 1)
    for k in range(max(0, per_dp - 2), per_dp):
        reduce_z(k)
    for r in range(cov_rows.shape[0] // per_dp):
        cov_out[:, pl.ds(r * 128, 128)] = cov_rows[pl.ds(r * per_dp, per_dp), :]
    for k in range(per_dp):
        for t in range(len(peers)):
            spec_copy(k, t).wait_send()
        y_copy(k).wait_send()
        for q in range(1, half):
            z_copy(k, q).wait_send()
        proj_copy(k).wait()


def body(n_order, n_dp, images, radial_interp, assignment, counts, radial_basis, eigenbasis):
    local_images, nodes, samples = images.shape
    slot_total = assignment.shape[0]
    slots, _, width = radial_basis.shape
    per_dp, half, chips = slots // n_dp, n_dp // 2, n_order // CORES
    placed = assignment.reshape(n_order, n_dp, per_dp).transpose(0, 2, 1)
    row_index = (
        placed[..., None] + slot_total * jnp.arange(2, dtype=jnp.int32)
    ).reshape(2 * slot_total, 1)
    mask = (jnp.arange(width, dtype=jnp.int32)[None, :] < counts[:, None]).astype(F32)
    mask = mask.reshape(slots, 1, width)
    base = jnp.asarray(base_table(slot_total, samples))
    block = 2 * n_dp * local_images
    n_peers = n_order - 1
    chip_rows = CORES * slots * 2
    parts = 4
    vmem = pl.BlockSpec(memory_space=pltpu.VMEM)
    any_space = pl.BlockSpec(memory_space=pl.ANY)
    dma = pltpu.SemaphoreType.DMA
    group = n_order * local_images
    covariance, projected = pl.pallas_call(
        functools.partial(kernel, n_order, n_dp),
        out_shape=(
            jax.ShapeDtypeStruct((per_dp, 2 * width * width), F32),
            jax.ShapeDtypeStruct((2, n_dp, per_dp, group, width), BF16),
        ),
        in_specs=[any_space, vmem, vmem, vmem, vmem, any_space, any_space],
        out_specs=(vmem, any_space),
        scratch_shapes=[
            pltpu.VMEM((local_images, nodes, samples), BF16),
            pltpu.VMEM((slots, nodes, width), BF16),
            pltpu.VMEM((slots, width, width), BF16),
            pltpu.VMEM((2 * slot_total, samples), BF16),
            pltpu.VMEM((slots, nodes, width), BF16),
            pltpu.VMEM((chip_rows * local_images, nodes), F32),
            pltpu.VMEM((n_peers, per_dp, block, nodes), BF16),
            pltpu.VMEM((per_dp, n_order, block, nodes), BF16),
            pltpu.VMEM((per_dp, 2, n_dp, group, width), BF16),
            pltpu.VMEM((per_dp, 2, half, width, width), BF16),
            pltpu.VMEM((per_dp, half, width, width), BF16),
            pltpu.VMEM((per_dp, half, width, width), BF16),
            pltpu.VMEM((per_dp, half, width, width), BF16),
            pltpu.VMEM((2 * width * per_dp, width), F32),
            dma((parts,)),
            dma((2,)),
            dma((n_peers, per_dp)),
            dma((n_peers, per_dp)),
            dma((per_dp,)),
            dma((per_dp,)),
            dma((per_dp, half)),
            dma((per_dp, half)),
            dma((per_dp,)),
        ],
        compiler_params=pltpu.CompilerParams(
            collective_id=0, has_side_effects=True, vmem_limit_bytes=60 * 2**20
        ),
        cost_estimate=pl.CostEstimate(
            flops=5_000_000_000, bytes_accessed=14_000_000, transcendentals=0
        ),
    )(images, radial_interp, row_index, base, mask, radial_basis, eigenbasis)
    return covariance, projected.reshape(2, slots, group, width)


def solution(mesh):
    placed = (
        P(("dp", "order"), None, None),
        P(),
        P(),
        P("order"),
        P("order", None, None),
        P("order", None, None),
    )
    return jax.shard_map(
        functools.partial(body, mesh.shape["order"], mesh.shape["dp"]),
        mesh=mesh,
        in_specs=placed,
        out_specs=(P(("order", "dp"), None), P(None, "order", "dp", None)),
        check_vma=False,
    )
```

```python
import functools
import math

import jax
import jax.numpy as jnp
import ml_dtypes
import numpy as np
from jax import lax
from jax.experimental import pallas as pl
from jax.experimental.pallas import tpu as pltpu
from jax.sharding import PartitionSpec as P

MESH = pl.DeviceIdType.MESH
BF16 = jnp.bfloat16
F32 = jnp.float32
CORES = 2
WINDOW = 2


def base_table(orders, samples):
    angle = (np.arange(orders)[:, None] * np.arange(samples)[None, :]) % samples
    theta = angle.astype(np.float32) * np.float32(2.0 * math.pi / samples)
    rows = np.concatenate([np.cos(theta), -np.sin(theta)], 0) / np.sqrt(np.float32(samples))
    return rows.astype(ml_dtypes.bfloat16)


def kernel(
    n_order, n_dp, images_hbm, interp_hbm, assignment, base_hbm, counts, basis_hbm, eigen_hbm,
    cov_out, proj_out,
    interp, base, images, basis, eigen, table, kept, wide, send, recv, proj, cov_own, cov_y, cov_z, cov_got,
    image_sem, weight_sem, spec_send, spec_recv, y_send, y_recv, z_send, z_recv, proj_sem,
):
    local_images, nodes, samples = images.shape
    slots = basis.shape[0]
    chips, half, per_dp = n_order // CORES, n_dp // 2, slots // n_dp
    chip_rows = CORES * slots * 2
    block = n_dp * local_images
    me, my_dp = lax.axis_index("order"), lax.axis_index("dp")
    my_chip, my_core = me // CORES, me % CORES
    my_z, my_y = my_dp // 2, my_dp % 2

    def order_of(dx, dc):
        return lax.rem(my_chip + dx, chips) * CORES + lax.rem(my_core + dc, CORES)

    peers = [(dx, dc) for dx in range(1, chips) for dc in range(CORES)] + [(0, 1)]
    y_peer = my_z * 2 + (1 - my_y)

    def z_peer(q):
        return lax.rem(my_z + q, half)

    barrier = pltpu.get_barrier_semaphore()
    for dx, dc in peers:
        pl.semaphore_signal(barrier, 1, device_id={"order": order_of(dx, dc)}, device_id_type=MESH)
    pl.semaphore_signal(barrier, 1, device_id={"dp": y_peer}, device_id_type=MESH)
    for q in range(1, half):
        pl.semaphore_signal(
            barrier, 1, device_id={"dp": z_peer(q) * 2 + my_y}, device_id_type=MESH
        )

    parts = image_sem.shape[0]
    per_part = local_images // parts
    image_copies = [
        pltpu.make_async_copy(
            images_hbm.at[pl.ds(n * per_part, per_part)],
            images.at[pl.ds(n * per_part, per_part)],
            image_sem.at[n],
        )
        for n in range(parts)
    ]
    base_copy = pltpu.make_async_copy(base_hbm, base, weight_sem.at[2])
    interp_copy = pltpu.make_async_copy(interp_hbm, interp, weight_sem.at[3])
    base_copy.start()
    for copy in image_copies:
        copy.start()
    interp_copy.start()
    basis_copy = pltpu.make_async_copy(basis_hbm, basis, weight_sem.at[0])
    eigen_copy = pltpu.make_async_copy(eigen_hbm, eigen, weight_sem.at[1])
    basis_copy.start()
    eigen_copy.start()

    total = n_order * slots
    row = lax.broadcasted_iota(jnp.int32, (total, total), 0)
    lane = lax.broadcasted_iota(jnp.int32, (total, total), 1)
    owner, chunk, dp_owner = lane // slots, (lane % slots) // n_dp, lane % n_dp
    to_row = row == owner * slots + dp_owner * per_dp + chunk
    is_order = row == assignment[...]
    pick = jnp.dot(
        is_order.astype(F32).astype(BF16),
        to_row.astype(F32).astype(BF16),
        preferred_element_type=F32,
    ).astype(BF16)
    base_copy.wait()
    for p in range(2):
        table[p] = lax.dot_general(
            pick, base[pl.ds(p * total, total), :],
            (((0,), (0,)), ((), ())), preferred_element_type=F32,
        ).astype(BF16)

    def transform(dx, first):
        start = pl.multiple_of(
            lax.rem(my_chip + dx, chips) * (chip_rows // 2), chip_rows // 2
        )
        rows = table[:, pl.ds(start, chip_rows // 2), :].reshape(chip_rows, samples)
        for n in range(parts):
            if first:
                image_copies[n].wait()

            @pl.loop(0, per_part // 2)
            def _(h):
                i = n * per_part + h * 2
                pair = images[pl.ds(i, 2)].reshape(2 * nodes, samples)
                got = lax.dot_general(
                    rows, pair,
                    (((1,), (1,)), ((), ())), preferred_element_type=F32,
                )
                wide[pl.ds(i, chip_rows, stride=local_images), :] = got[:, :nodes]
                wide[pl.ds(i + 1, chip_rows, stride=local_images), :] = got[:, nodes:]

    def spec_copy(k, t):
        dx, dc = peers[t]
        return pltpu.make_async_remote_copy(
            src_ref=send.at[t, k],
            dst_ref=recv.at[k, me],
            send_sem=spec_send.at[t, k],
            recv_sem=spec_recv.at[t, k],
            device_id={"order": order_of(dx, dc)},
            device_id_type=MESH,
        )

    def narrowed(dc, k, p):
        core = lax.rem(my_core + dc, CORES)
        at = pl.multiple_of(((p * CORES + core) * per_dp + k) * block, block)
        return wide[pl.ds(at, block), :].astype(BF16)

    far = len(peers) - 1
    for dx in range(1, chips):
        transform(dx, dx == 1)
        if dx == 1:
            pl.semaphore_wait(barrier, len(peers) + half)
        for k in range(per_dp):
            for dc in range(CORES):
                t = (dx - 1) * CORES + dc
                for p in range(2):
                    send[t, k, p] = narrowed(dc, k, p)
                if k < WINDOW:
                    spec_copy(k, t).start()
    transform(0, chips == 1)
    for k in range(per_dp):
        for p in range(2):
            send[far, k, p] = narrowed(1, k, p)
        spec_copy(k, far).start()
    for k in range(per_dp):
        for p in range(2):
            recv[k, me, p] = narrowed(0, k, p)

    basis_copy.wait()
    interp_copy.wait()
    column = lax.broadcasted_iota(jnp.int32, (1, kept.shape[2]), 1)

    @pl.loop(0, slots)
    def _(j):
        folded = jnp.dot(interp[...], basis[j], preferred_element_type=F32)
        kept[j] = jnp.where(column < counts[j], folded, 0.0).astype(BF16)

    eigen_copy.wait()
    scale = 1.0 / (local_images * n_order * n_dp)

    def y_copy(k):
        return pltpu.make_async_remote_copy(
            src_ref=cov_own.at[k, 1 - my_y],
            dst_ref=cov_y.at[k],
            send_sem=y_send.at[k],
            recv_sem=y_recv.at[k],
            device_id={"dp": y_peer},
            device_id_type=MESH,
        )

    def z_copy(k, q):
        return pltpu.make_async_remote_copy(
            src_ref=cov_z.at[k, z_peer(q)],
            dst_ref=cov_got.at[k, q],
            send_sem=z_send.at[k, q],
            recv_sem=z_recv.at[k, q],
            device_id={"dp": z_peer(q) * 2 + my_y},
            device_id_type=MESH,
        )

    def proj_copy(k):
        return pltpu.make_async_copy(proj.at[k], proj_out.at[:, :, k], proj_sem.at[k])

    def slot_work(k):
        @pl.loop(0, half)
        def _(z):
            for y in range(2):
                d = z * 2 + y
                j = d * per_dp + k
                at = pl.multiple_of(d * local_images, local_images)
                both = jnp.concatenate(
                    [
                        recv[k, :, p, pl.ds(at, local_images), :].reshape(
                            n_order * local_images, nodes
                        )
                        for p in range(2)
                    ],
                    0,
                )
                coef = jnp.dot(both, kept[j], preferred_element_type=F32).astype(BF16)
                real, imag = coef[: n_order * local_images], coef[n_order * local_images :]
                mixed = jnp.concatenate([real - imag, real + imag], 0)
                cov = lax.dot_general(
                    coef, mixed, (((0,), (0,)), ((), ())), preferred_element_type=F32
                )
                cov_own[k, y, z] = (cov * scale).astype(BF16)
                out = jnp.dot(coef, eigen[j], preferred_element_type=F32).astype(BF16)
                proj[k, 0, d] = out[: n_order * local_images]
                proj[k, 1, d] = out[n_order * local_images :]

    def reduce_y(k):
        y_copy(k).wait_recv()
        cov_z[k] = (cov_own[k, my_y].astype(F32) + cov_y[k].astype(F32)).astype(BF16)
        for q in range(1, half):
            z_copy(k, q).start()

    def reduce_z(k):
        whole = cov_z[k, my_z].astype(F32)
        for q in range(1, half):
            z_copy(k, q).wait_recv()
            whole = whole + cov_got[k, q].astype(F32)
        cov_out[k] = whole

    for k in range(per_dp):
        for t in range(len(peers)):
            spec_copy(k, t).wait_recv()
        if k + WINDOW < per_dp:
            for t in range(far):
                spec_copy(k + WINDOW, t).start()
        slot_work(k)
        y_copy(k).start()
        proj_copy(k).start()
        if k >= 1:
            reduce_y(k - 1)
        if k >= 2:
            reduce_z(k - 2)
    reduce_y(per_dp - 1)
    for k in range(max(0, per_dp - 2), per_dp):
        reduce_z(k)
    for k in range(per_dp):
        for t in range(len(peers)):
            spec_copy(k, t).wait_send()
        y_copy(k).wait_send()
        for q in range(1, half):
            z_copy(k, q).wait_send()
        proj_copy(k).wait()


def finish(whole, proj, cov_out, proj_out, rows, sems):
    parts = [(p, z) for p in range(2) for z in range(sems.shape[1])]
    size = proj.shape[1] // sems.shape[1]
    copies = [
        pltpu.make_async_copy(
            proj.at[p, pl.ds(z * size, size)], proj_out.at[p, pl.ds(z * size, size)], sems.at[p, z]
        )
        for p, z in parts
    ]
    for copy in copies:
        copy.start()
    slots, width, _ = whole.shape
    for k in range(slots):
        one = whole[k]
        flipped = one.T
        rows[pl.ds(k, width, stride=slots), :] = (one + flipped) * 0.5
        rows[pl.ds(width * slots + k, width, stride=slots), :] = (one - flipped) * 0.5
    for r in range(2 * width):
        cov_out[:, pl.ds(r * width, width)] = rows[pl.ds(r * slots, slots), :]
    for copy in copies:
        copy.wait()


def body(n_order, n_dp, images, radial_interp, assignment, counts, radial_basis, eigenbasis):
    local_images, nodes, samples = images.shape
    slot_total = assignment.shape[0]
    slots, _, width = radial_basis.shape
    per_dp, half, chips = slots // n_dp, n_dp // 2, n_order // CORES
    base = jnp.asarray(base_table(slot_total, samples))
    block = n_dp * local_images
    n_peers = n_order - 1
    chip_rows = CORES * slots * 2
    parts = 4
    vmem = pl.BlockSpec(memory_space=pltpu.VMEM)
    any_space = pl.BlockSpec(memory_space=pl.ANY)
    hbm = pl.BlockSpec(memory_space=pltpu.HBM)
    dma = pltpu.SemaphoreType.DMA
    group = n_order * local_images
    whole, projected = pl.pallas_call(
        functools.partial(kernel, n_order, n_dp),
        out_shape=(
            jax.ShapeDtypeStruct((per_dp, width, width), F32),
            jax.ShapeDtypeStruct((2, n_dp, per_dp, group, width), BF16),
        ),
        in_specs=[
            hbm, hbm, vmem, hbm, pl.BlockSpec(memory_space=pltpu.SMEM),
            hbm, hbm,
        ],
        out_specs=(vmem, any_space),
        scratch_shapes=[
            pltpu.VMEM((nodes, nodes), BF16),
            pltpu.VMEM((2 * slot_total, samples), BF16),
            pltpu.VMEM((local_images, nodes, samples), BF16),
            pltpu.VMEM((slots, nodes, width), BF16),
            pltpu.VMEM((slots, width, width), BF16),
            pltpu.VMEM((2, slot_total, samples), BF16),
            pltpu.VMEM((slots, nodes, width), BF16),
            pltpu.VMEM((chip_rows * local_images, nodes), F32),
            pltpu.VMEM((n_peers, per_dp, 2, block, nodes), BF16),
            pltpu.VMEM((per_dp, n_order, 2, block, nodes), BF16),
            pltpu.VMEM((per_dp, 2, n_dp, group, width), BF16),
            pltpu.VMEM((per_dp, 2, half, width, width), BF16),
            pltpu.VMEM((per_dp, half, width, width), BF16),
            pltpu.VMEM((per_dp, half, width, width), BF16),
            pltpu.VMEM((per_dp, half, width, width), BF16),
            dma((parts,)),
            dma((4,)),
            dma((n_peers, per_dp)),
            dma((n_peers, per_dp)),
            dma((per_dp,)),
            dma((per_dp,)),
            dma((per_dp, half)),
            dma((per_dp, half)),
            dma((per_dp,)),
        ],
        compiler_params=pltpu.CompilerParams(
            collective_id=0, has_side_effects=True, vmem_limit_bytes=44 * 2**20
        ),
        cost_estimate=pl.CostEstimate(
            flops=5_000_000_000, bytes_accessed=14_000_000, transcendentals=0
        ),
    )(images, radial_interp, assignment.reshape(1, -1), base, counts, radial_basis, eigenbasis)
    projected = projected.reshape(2, slots, group, width)
    return pl.pallas_call(
        finish,
        out_shape=(
            jax.ShapeDtypeStruct((per_dp, 2 * width * width), F32),
            jax.ShapeDtypeStruct(projected.shape, BF16),
        ),
        in_specs=[vmem, any_space],
        out_specs=(vmem, any_space),
        scratch_shapes=[pltpu.VMEM((2 * width * per_dp, width), F32), dma((2, 4))],
        compiler_params=pltpu.CompilerParams(vmem_limit_bytes=16 * 2**20),
        cost_estimate=pl.CostEstimate(
            flops=1_000_000, bytes_accessed=10_000_000, transcendentals=0
        ),
    )(whole, projected)


def solution(mesh):
    placed = (
        P(("dp", "order"), None, None),
        P(),
        P(),
        P("order"),
        P("order", None, None),
        P("order", None, None),
    )
    return jax.shard_map(
        functools.partial(body, mesh.shape["order"], mesh.shape["dp"]),
        mesh=mesh,
        in_specs=placed,
        out_specs=(P(("order", "dp"), None), P(None, "order", "dp", None)),
        check_vma=False,
    )
```

```python
import functools
import math

import jax
import jax.numpy as jnp
import ml_dtypes
import numpy as np
from jax import lax
from jax.experimental import pallas as pl
from jax.experimental.pallas import tpu as pltpu
from jax.sharding import PartitionSpec as P

MESH = pl.DeviceIdType.MESH
BF16 = jnp.bfloat16
F32 = jnp.float32
CORES = 2
WINDOW = 8


def base_table(orders, samples):
    angle = (np.arange(orders)[:, None] * np.arange(samples)[None, :]) % samples
    theta = angle.astype(np.float32) * np.float32(2.0 * math.pi / samples)
    rows = np.concatenate([np.cos(theta), -np.sin(theta)], 0) / np.sqrt(np.float32(samples))
    return rows.astype(ml_dtypes.bfloat16)


def kernel(
    n_order, n_dp, images_hbm, interp_hbm, assignment_hbm, base_hbm, counts_hbm, basis_hbm, eigen_hbm,
    cov_out, proj_out,
    assignment, counts, interp, base, images, basis, eigen, table, kept, wide, send, recv, proj, cov_own, cov_y, cov_z, cov_got,
    image_sem, weight_sem, spec_send, spec_recv, y_send, y_recv, z_send, z_recv, proj_sem,
):
    local_images, nodes, samples = images.shape
    slots = basis.shape[0]
    chips, half, per_dp = n_order // CORES, n_dp // 2, slots // n_dp
    chip_rows = CORES * slots * 2
    block = n_dp * local_images
    me, my_dp = lax.axis_index("order"), lax.axis_index("dp")
    my_chip, my_core = me // CORES, me % CORES
    my_z, my_y = my_dp // 2, my_dp % 2

    def order_of(dx, dc):
        return lax.rem(my_chip + dx, chips) * CORES + lax.rem(my_core + dc, CORES)

    peers = [(dx, dc) for dx in range(1, chips) for dc in range(CORES)] + [(0, 1)]
    y_peer = my_z * 2 + (1 - my_y)

    def z_peer(q):
        return lax.rem(my_z + q, half)

    barrier = pltpu.get_barrier_semaphore()
    for dx, dc in peers:
        pl.semaphore_signal(barrier, 1, device_id={"order": order_of(dx, dc)}, device_id_type=MESH)
    pl.semaphore_signal(barrier, 1, device_id={"dp": y_peer}, device_id_type=MESH)
    for q in range(1, half):
        pl.semaphore_signal(
            barrier, 1, device_id={"dp": z_peer(q) * 2 + my_y}, device_id_type=MESH
        )

    parts = image_sem.shape[0]
    per_part = local_images // parts
    image_copies = [
        pltpu.make_async_copy(
            images_hbm.at[pl.ds(n * per_part, per_part)],
            images.at[pl.ds(n * per_part, per_part)],
            image_sem.at[n],
        )
        for n in range(parts)
    ]
    base_copy = pltpu.make_async_copy(base_hbm, base, weight_sem.at[2])
    interp_copy = pltpu.make_async_copy(interp_hbm, interp, weight_sem.at[3])
    assignment_copy = pltpu.make_async_copy(assignment_hbm, assignment, weight_sem.at[4])
    counts_copy = pltpu.make_async_copy(counts_hbm, counts, weight_sem.at[5])
    assignment_copy.start()
    counts_copy.start()
    base_copy.start()
    for copy in image_copies:
        copy.start()
    interp_copy.start()
    basis_copy = pltpu.make_async_copy(basis_hbm, basis, weight_sem.at[0])
    eigen_copy = pltpu.make_async_copy(eigen_hbm, eigen, weight_sem.at[1])
    basis_copy.start()
    eigen_copy.start()

    total = n_order * slots
    row = lax.broadcasted_iota(jnp.int32, (total, total), 0)
    lane = lax.broadcasted_iota(jnp.int32, (total, total), 1)
    owner, chunk, dp_owner = lane // slots, (lane % slots) // n_dp, lane % n_dp
    to_row = row == owner * slots + dp_owner * per_dp + chunk
    assignment_copy.wait()
    is_order = row == assignment[...]
    pick = jnp.dot(
        is_order.astype(F32).astype(BF16),
        to_row.astype(F32).astype(BF16),
        preferred_element_type=F32,
    ).astype(BF16)
    base_copy.wait()
    for p in range(2):
        table[p] = lax.dot_general(
            pick, base[pl.ds(p * total, total), :],
            (((0,), (0,)), ((), ())), preferred_element_type=F32,
        ).astype(BF16)

    def transform(dx, first):
        start = pl.multiple_of(
            lax.rem(my_chip + dx, chips) * (chip_rows // 2), chip_rows // 2
        )
        rows = table[:, pl.ds(start, chip_rows // 2), :].reshape(chip_rows, samples)
        for n in range(parts):
            if first:
                image_copies[n].wait()

            @pl.loop(0, per_part // 2)
            def _(h):
                i = n * per_part + h * 2
                pair = images[pl.ds(i, 2)].reshape(2 * nodes, samples)
                got = lax.dot_general(
                    rows, pair,
                    (((1,), (1,)), ((), ())), preferred_element_type=F32,
                )
                wide[pl.ds(i, chip_rows, stride=local_images), :] = got[:, :nodes]
                wide[pl.ds(i + 1, chip_rows, stride=local_images), :] = got[:, nodes:]

    def spec_copy(k, t):
        dx, dc = peers[t]
        return pltpu.make_async_remote_copy(
            src_ref=send.at[t, k],
            dst_ref=recv.at[k, me],
            send_sem=spec_send.at[t, k],
            recv_sem=spec_recv.at[t, k],
            device_id={"order": order_of(dx, dc)},
            device_id_type=MESH,
        )

    def narrowed(dc, k, p):
        core = lax.rem(my_core + dc, CORES)
        at = pl.multiple_of(((p * CORES + core) * per_dp + k) * block, block)
        return wide[pl.ds(at, block), :].astype(BF16)

    far = len(peers) - 1
    for dx in range(1, chips):
        transform(dx, dx == 1)
        if dx == 1:
            pl.semaphore_wait(barrier, len(peers) + half)
        for k in range(per_dp):
            for dc in range(CORES):
                t = (dx - 1) * CORES + dc
                for p in range(2):
                    send[t, k, p] = narrowed(dc, k, p)
                if k < WINDOW:
                    spec_copy(k, t).start()
    transform(0, chips == 1)
    for k in range(per_dp):
        for p in range(2):
            send[far, k, p] = narrowed(1, k, p)
        spec_copy(k, far).start()
    for k in range(per_dp):
        for p in range(2):
            recv[k, me, p] = narrowed(0, k, p)

    basis_copy.wait()
    interp_copy.wait()
    counts_copy.wait()
    column = lax.broadcasted_iota(jnp.int32, (1, kept.shape[2]), 1)

    @pl.loop(0, slots)
    def _(j):
        folded = jnp.dot(interp[...], basis[j], preferred_element_type=F32)
        kept[j] = jnp.where(column < counts[j], folded, 0.0).astype(BF16)

    eigen_copy.wait()
    scale = 1.0 / (local_images * n_order * n_dp)

    def y_copy(k):
        return pltpu.make_async_remote_copy(
            src_ref=cov_own.at[k, 1 - my_y],
            dst_ref=cov_y.at[k],
            send_sem=y_send.at[k],
            recv_sem=y_recv.at[k],
            device_id={"dp": y_peer},
            device_id_type=MESH,
        )

    def z_copy(k, q):
        return pltpu.make_async_remote_copy(
            src_ref=cov_z.at[k, z_peer(q)],
            dst_ref=cov_got.at[k, q],
            send_sem=z_send.at[k, q],
            recv_sem=z_recv.at[k, q],
            device_id={"dp": z_peer(q) * 2 + my_y},
            device_id_type=MESH,
        )

    def proj_copy(k):
        return pltpu.make_async_copy(proj.at[k], proj_out.at[:, :, k], proj_sem.at[k])

    def slot_work(k):
        @pl.loop(0, half)
        def _(z):
            for y in range(2):
                d = z * 2 + y
                j = d * per_dp + k
                at = pl.multiple_of(d * local_images, local_images)
                both = jnp.concatenate(
                    [
                        recv[k, :, p, pl.ds(at, local_images), :].reshape(
                            n_order * local_images, nodes
                        )
                        for p in range(2)
                    ],
                    0,
                )
                coef = jnp.dot(both, kept[j], preferred_element_type=F32).astype(BF16)
                real, imag = coef[: n_order * local_images], coef[n_order * local_images :]
                mixed = jnp.concatenate([real - imag, real + imag], 0)
                cov = lax.dot_general(
                    coef, mixed, (((0,), (0,)), ((), ())), preferred_element_type=F32
                )
                cov_own[k, y, z] = (cov * scale).astype(BF16)
                out = jnp.dot(coef, eigen[j], preferred_element_type=F32).astype(BF16)
                proj[k, 0, d] = out[: n_order * local_images]
                proj[k, 1, d] = out[n_order * local_images :]

    def reduce_y(k):
        y_copy(k).wait_recv()
        cov_z[k] = (cov_own[k, my_y].astype(F32) + cov_y[k].astype(F32)).astype(BF16)
        for q in range(1, half):
            z_copy(k, q).start()

    def reduce_z(k):
        whole = cov_z[k, my_z].astype(F32)
        for q in range(1, half):
            z_copy(k, q).wait_recv()
            whole = whole + cov_got[k, q].astype(F32)
        cov_out[k] = whole

    for k in range(per_dp):
        for t in range(len(peers)):
            spec_copy(k, t).wait_recv()
        if k + WINDOW < per_dp:
            for t in range(far):
                spec_copy(k + WINDOW, t).start()
        slot_work(k)
        y_copy(k).start()
        proj_copy(k).start()
        if k >= 1:
            reduce_y(k - 1)
        if k >= 2:
            reduce_z(k - 2)
    reduce_y(per_dp - 1)
    for k in range(max(0, per_dp - 2), per_dp):
        reduce_z(k)
    for k in range(per_dp):
        for t in range(len(peers)):
            spec_copy(k, t).wait_send()
        y_copy(k).wait_send()
        for q in range(1, half):
            z_copy(k, q).wait_send()
        proj_copy(k).wait()


def finish(whole, proj, cov_out, proj_out, rows, sems):
    parts = [(p, z) for p in range(2) for z in range(sems.shape[1])]
    size = proj.shape[1] // sems.shape[1]
    copies = [
        pltpu.make_async_copy(
            proj.at[p, pl.ds(z * size, size)], proj_out.at[p, pl.ds(z * size, size)], sems.at[p, z]
        )
        for p, z in parts
    ]
    for copy in copies:
        copy.start()
    slots, width, _ = whole.shape
    for k in range(slots):
        one = whole[k]
        flipped = one.T
        rows[pl.ds(k, width, stride=slots), :] = (one + flipped) * 0.5
        rows[pl.ds(width * slots + k, width, stride=slots), :] = (one - flipped) * 0.5
    for r in range(2 * width):
        cov_out[:, pl.ds(r * width, width)] = rows[pl.ds(r * slots, slots), :]
    for copy in copies:
        copy.wait()


def body(n_order, n_dp, images, radial_interp, assignment, counts, radial_basis, eigenbasis):
    local_images, nodes, samples = images.shape
    slot_total = assignment.shape[0]
    slots, _, width = radial_basis.shape
    per_dp, half, chips = slots // n_dp, n_dp // 2, n_order // CORES
    base = jnp.asarray(base_table(slot_total, samples))
    block = n_dp * local_images
    n_peers = n_order - 1
    chip_rows = CORES * slots * 2
    parts = 4
    in_hbm = functools.partial(pltpu.with_memory_space_constraint, memory_space=pltpu.HBM)
    vmem = pl.BlockSpec(memory_space=pltpu.VMEM)
    any_space = pl.BlockSpec(memory_space=pl.ANY)
    hbm = pl.BlockSpec(memory_space=pltpu.HBM)
    dma = pltpu.SemaphoreType.DMA
    group = n_order * local_images
    whole, projected = pl.pallas_call(
        functools.partial(kernel, n_order, n_dp),
        out_shape=(
            jax.ShapeDtypeStruct((per_dp, width, width), F32),
            jax.ShapeDtypeStruct((2, n_dp, per_dp, group, width), BF16),
        ),
        in_specs=[hbm] * 7,
        out_specs=(vmem, any_space),
        scratch_shapes=[
            pltpu.VMEM((1, slot_total), jnp.int32),
            pltpu.SMEM((slots,), jnp.int32),
            pltpu.VMEM((nodes, nodes), BF16),
            pltpu.VMEM((2 * slot_total, samples), BF16),
            pltpu.VMEM((local_images, nodes, samples), BF16),
            pltpu.VMEM((slots, nodes, width), BF16),
            pltpu.VMEM((slots, width, width), BF16),
            pltpu.VMEM((2, slot_total, samples), BF16),
            pltpu.VMEM((slots, nodes, width), BF16),
            pltpu.VMEM((chip_rows * local_images, nodes), F32),
            pltpu.VMEM((n_peers, per_dp, 2, block, nodes), BF16),
            pltpu.VMEM((per_dp, n_order, 2, block, nodes), BF16),
            pltpu.VMEM((per_dp, 2, n_dp, group, width), BF16),
            pltpu.VMEM((per_dp, 2, half, width, width), BF16),
            pltpu.VMEM((per_dp, half, width, width), BF16),
            pltpu.VMEM((per_dp, half, width, width), BF16),
            pltpu.VMEM((per_dp, half, width, width), BF16),
            dma((parts,)),
            dma((6,)),
            dma((n_peers, per_dp)),
            dma((n_peers, per_dp)),
            dma((per_dp,)),
            dma((per_dp,)),
            dma((per_dp, half)),
            dma((per_dp, half)),
            dma((per_dp,)),
        ],
        compiler_params=pltpu.CompilerParams(
            collective_id=0, has_side_effects=True, vmem_limit_bytes=44 * 2**20
        ),
        cost_estimate=pl.CostEstimate(
            flops=5_000_000_000, bytes_accessed=14_000_000, transcendentals=0
        ),
    )(
        *map(
            in_hbm,
            (
                images, radial_interp, assignment.reshape(1, -1), base, counts,
                radial_basis, eigenbasis,
            ),
        )
    )
    projected = projected.reshape(2, slots, group, width)
    return pl.pallas_call(
        finish,
        out_shape=(
            jax.ShapeDtypeStruct((per_dp, 2 * width * width), F32),
            jax.ShapeDtypeStruct(projected.shape, BF16),
        ),
        in_specs=[vmem, any_space],
        out_specs=(vmem, any_space),
        scratch_shapes=[pltpu.VMEM((2 * width * per_dp, width), F32), dma((2, 4))],
        compiler_params=pltpu.CompilerParams(vmem_limit_bytes=16 * 2**20),
        cost_estimate=pl.CostEstimate(
            flops=1_000_000, bytes_accessed=10_000_000, transcendentals=0
        ),
    )(whole, projected)


def solution(mesh):
    placed = (
        P(("dp", "order"), None, None),
        P(),
        P(),
        P("order"),
        P("order", None, None),
        P("order", None, None),
    )
    return jax.shard_map(
        functools.partial(body, mesh.shape["order"], mesh.shape["dp"]),
        mesh=mesh,
        in_specs=placed,
        out_specs=(P(("order", "dp"), None), P(None, "order", "dp", None)),
        check_vma=False,
    )
```

```python
import functools
import math

import jax
import jax.numpy as jnp
import ml_dtypes
import numpy as np
from jax import lax
from jax.experimental import pallas as pl
from jax.experimental.pallas import tpu as pltpu
from jax.sharding import PartitionSpec as P

MESH = pl.DeviceIdType.MESH
BF16 = jnp.bfloat16
F32 = jnp.float32
CORES = 2


def base_table(orders, samples):
    angle = (np.arange(orders)[:, None] * np.arange(samples)[None, :]) % samples
    theta = angle.astype(np.float32) * np.float32(2.0 * math.pi / samples)
    rows = np.concatenate([np.cos(theta), -np.sin(theta)], 0) / np.sqrt(np.float32(samples))
    return rows.astype(ml_dtypes.bfloat16)


def kernel(
    n_order, n_dp, images_hbm, interp_hbm, assignment_hbm, base_hbm, counts_hbm, basis_hbm, eigen_hbm,
    cov_out, proj_out,
    assignment, counts, interp, base, images, basis, eigen, table, kept, wide, send, recv, proj, cov_own, cov_y, cov_z, cov_got,
    image_sem, weight_sem, spec_send, spec_recv, y_send, y_recv, z_send, z_recv, proj_sem,
):
    local_images, nodes, samples = images.shape
    slots = basis.shape[0]
    chips, half, per_dp = n_order // CORES, n_dp // 2, slots // n_dp
    chip_rows = CORES * slots * 2
    block = n_dp * local_images
    me, my_dp = lax.axis_index("order"), lax.axis_index("dp")
    my_chip, my_core = me // CORES, me % CORES
    my_z, my_y = my_dp // 2, my_dp % 2

    def order_of(dx, dc):
        return lax.rem(my_chip + dx, chips) * CORES + lax.rem(my_core + dc, CORES)

    peers = [(dx, dc) for dx in range(1, chips) for dc in range(CORES)] + [(0, 1)]
    y_peer = my_z * 2 + (1 - my_y)

    def z_peer(q):
        return lax.rem(my_z + q, half)

    barrier = pltpu.get_barrier_semaphore()
    for dx, dc in peers:
        pl.semaphore_signal(barrier, 1, device_id={"order": order_of(dx, dc)}, device_id_type=MESH)
    pl.semaphore_signal(barrier, 1, device_id={"dp": y_peer}, device_id_type=MESH)
    for q in range(1, half):
        pl.semaphore_signal(
            barrier, 1, device_id={"dp": z_peer(q) * 2 + my_y}, device_id_type=MESH
        )

    parts = image_sem.shape[0]
    per_part = local_images // parts
    image_copies = [
        pltpu.make_async_copy(
            images_hbm.at[pl.ds(n * per_part, per_part)],
            images.at[pl.ds(n * per_part, per_part)],
            image_sem.at[n],
        )
        for n in range(parts)
    ]
    base_copy = pltpu.make_async_copy(base_hbm, base, weight_sem.at[2])
    interp_copy = pltpu.make_async_copy(interp_hbm, interp, weight_sem.at[3])
    assignment_copy = pltpu.make_async_copy(assignment_hbm, assignment, weight_sem.at[4])
    counts_copy = pltpu.make_async_copy(counts_hbm, counts, weight_sem.at[5])
    assignment_copy.start()
    counts_copy.start()
    base_copy.start()
    for copy in image_copies:
        copy.start()
    interp_copy.start()
    basis_copy = pltpu.make_async_copy(basis_hbm, basis, weight_sem.at[0])
    eigen_copy = pltpu.make_async_copy(eigen_hbm, eigen, weight_sem.at[1])
    basis_copy.start()
    eigen_copy.start()

    total = n_order * slots
    row = lax.broadcasted_iota(jnp.int32, (total, total), 0)
    lane = lax.broadcasted_iota(jnp.int32, (total, total), 1)
    step = n_dp * CORES
    chip, chunk = lane // (step * per_dp), (lane // step) % per_dp
    core, dp_owner = (lane // n_dp) % CORES, lane % n_dp
    to_row = row == (chip * CORES + core) * slots + dp_owner * per_dp + chunk
    assignment_copy.wait()
    is_order = row == assignment[...]
    pick = jnp.dot(
        is_order.astype(F32).astype(BF16),
        to_row.astype(F32).astype(BF16),
        preferred_element_type=F32,
    ).astype(BF16)
    base_copy.wait()
    for p in range(2):
        table[p] = lax.dot_general(
            pick, base[pl.ds(p * total, total), :],
            (((0,), (0,)), ((), ())), preferred_element_type=F32,
        ).astype(BF16)

    def transform(dx, k0, k1, first):
        at = lax.rem(my_chip + dx, chips) * (step * per_dp) + k0 * step
        count = (k1 - k0) * step
        rows = table[:, pl.ds(pl.multiple_of(at, step), count), :].reshape(2 * count, samples)
        for n in range(parts):
            if first:
                image_copies[n].wait()

            @pl.loop(0, per_part // 2)
            def _(h):
                i = n * per_part + h * 2
                pair = images[pl.ds(i, 2)].reshape(2 * nodes, samples)
                got = lax.dot_general(
                    rows, pair,
                    (((1,), (1,)), ((), ())), preferred_element_type=F32,
                )
                wide[pl.ds(i, 2 * count, stride=local_images), :] = got[:, :nodes]
                wide[pl.ds(i + 1, 2 * count, stride=local_images), :] = got[:, nodes:]

    def spec_copy(k, t):
        dx, dc = peers[t]
        return pltpu.make_async_remote_copy(
            src_ref=send.at[t, k],
            dst_ref=recv.at[k, me],
            send_sem=spec_send.at[t, k],
            recv_sem=spec_recv.at[t, k],
            device_id={"order": order_of(dx, dc)},
            device_id_type=MESH,
        )

    def narrowed(dc, k, k0, k1, p):
        core = lax.rem(my_core + dc, CORES)
        at = pl.multiple_of(((p * (k1 - k0) + k - k0) * CORES + core) * block, block)
        return wide[pl.ds(at, block), :].astype(BF16)

    far = len(peers) - 1
    groups = [(0, 2), (2, per_dp)] if per_dp > 2 else [(0, per_dp)]
    for dx in range(1, chips):
        for k0, k1 in groups:
            transform(dx, k0, k1, dx == 1 and k0 == 0)
            if dx == 1 and k0 == 0:
                pl.semaphore_wait(barrier, len(peers) + half)
            for k in range(k0, k1):
                for dc in range(CORES):
                    t = (dx - 1) * CORES + dc
                    for p in range(2):
                        send[t, k, p] = narrowed(dc, k, k0, k1, p)
                    spec_copy(k, t).start()
    transform(0, 0, per_dp, chips == 1)
    for k in range(per_dp):
        for p in range(2):
            send[far, k, p] = narrowed(1, k, 0, per_dp, p)
        spec_copy(k, far).start()
    for k in range(per_dp):
        for p in range(2):
            recv[k, me, p] = narrowed(0, k, 0, per_dp, p)

    basis_copy.wait()
    interp_copy.wait()
    counts_copy.wait()
    column = lax.broadcasted_iota(jnp.int32, (1, kept.shape[2]), 1)

    @pl.loop(0, slots)
    def _(j):
        folded = jnp.dot(interp[...], basis[j], preferred_element_type=F32)
        kept[j] = jnp.where(column < counts[j], folded, 0.0).astype(BF16)

    eigen_copy.wait()
    scale = 1.0 / (local_images * n_order * n_dp)

    def y_copy(k):
        return pltpu.make_async_remote_copy(
            src_ref=cov_own.at[k, 1 - my_y],
            dst_ref=cov_y.at[k],
            send_sem=y_send.at[k],
            recv_sem=y_recv.at[k],
            device_id={"dp": y_peer},
            device_id_type=MESH,
        )

    def z_copy(k, q):
        return pltpu.make_async_remote_copy(
            src_ref=cov_z.at[k, z_peer(q)],
            dst_ref=cov_got.at[k, q],
            send_sem=z_send.at[k, q],
            recv_sem=z_recv.at[k, q],
            device_id={"dp": z_peer(q) * 2 + my_y},
            device_id_type=MESH,
        )

    def proj_copy(k):
        return pltpu.make_async_copy(proj.at[k], proj_out.at[:, :, k], proj_sem.at[k])

    def slot_work(k, y):
        @pl.loop(0, half // 2)
        def _(h):
            for z in (h * 2, h * 2 + 1):
                d = z * 2 + y
                j = d * per_dp + k
                at = pl.multiple_of(d * local_images, local_images)
                both = jnp.concatenate(
                    [
                        recv[k, :, p, pl.ds(at, local_images), :].reshape(
                            n_order * local_images, nodes
                        )
                        for p in range(2)
                    ],
                    0,
                )
                coef = jnp.dot(both, kept[j], preferred_element_type=F32).astype(BF16)
                real, imag = coef[: n_order * local_images], coef[n_order * local_images :]
                mixed = jnp.concatenate([real - imag, real + imag], 0)
                cov = lax.dot_general(
                    coef, mixed, (((0,), (0,)), ((), ())), preferred_element_type=F32
                )
                cov_own[k, y, z] = (cov * scale).astype(BF16)
                out = jnp.dot(coef, eigen[j], preferred_element_type=F32).astype(BF16)
                proj[k, 0, d] = out[: n_order * local_images]
                proj[k, 1, d] = out[n_order * local_images :]

    def reduce_y(k):
        y_copy(k).wait_recv()
        cov_z[k] = (cov_own[k, my_y].astype(F32) + cov_y[k].astype(F32)).astype(BF16)
        for q in range(1, half):
            z_copy(k, q).start()

    def reduce_z(k):
        whole = cov_z[k, my_z].astype(F32)
        for q in range(1, half):
            z_copy(k, q).wait_recv()
            whole = whole + cov_got[k, q].astype(F32)
        cov_out[k] = whole

    for k in range(per_dp):
        for t in range(len(peers)):
            spec_copy(k, t).wait_recv()
        slot_work(k, 1 - my_y)
        y_copy(k).start()
        slot_work(k, my_y)
        proj_copy(k).start()
        if k >= 1:
            reduce_y(k - 1)
        if k >= 2:
            reduce_z(k - 2)
    reduce_y(per_dp - 1)
    for k in range(max(0, per_dp - 2), per_dp):
        reduce_z(k)
    for k in range(per_dp):
        for t in range(len(peers)):
            spec_copy(k, t).wait_send()
        y_copy(k).wait_send()
        for q in range(1, half):
            z_copy(k, q).wait_send()
        proj_copy(k).wait()


def finish(whole, proj, cov_out, proj_out, rows, sems):
    parts = [(p, z) for p in range(2) for z in range(sems.shape[1])]
    size = proj.shape[1] // sems.shape[1]
    copies = [
        pltpu.make_async_copy(
            proj.at[p, pl.ds(z * size, size)], proj_out.at[p, pl.ds(z * size, size)], sems.at[p, z]
        )
        for p, z in parts
    ]
    for copy in copies:
        copy.start()
    slots, width, _ = whole.shape
    for k in range(slots):
        one = whole[k]
        flipped = one.T
        rows[pl.ds(k, width, stride=slots), :] = (one + flipped) * 0.5
        rows[pl.ds(width * slots + k, width, stride=slots), :] = (one - flipped) * 0.5
    for r in range(2 * width):
        cov_out[:, pl.ds(r * width, width)] = rows[pl.ds(r * slots, slots), :]
    for copy in copies:
        copy.wait()


def body(n_order, n_dp, images, radial_interp, assignment, counts, radial_basis, eigenbasis):
    local_images, nodes, samples = images.shape
    slot_total = assignment.shape[0]
    slots, _, width = radial_basis.shape
    per_dp, half, chips = slots // n_dp, n_dp // 2, n_order // CORES
    base = jnp.asarray(base_table(slot_total, samples))
    block = n_dp * local_images
    n_peers = n_order - 1
    chip_rows = CORES * slots * 2
    parts = 4
    in_hbm = functools.partial(pltpu.with_memory_space_constraint, memory_space=pltpu.HBM)
    vmem = pl.BlockSpec(memory_space=pltpu.VMEM)
    any_space = pl.BlockSpec(memory_space=pl.ANY)
    hbm = pl.BlockSpec(memory_space=pltpu.HBM)
    dma = pltpu.SemaphoreType.DMA
    group = n_order * local_images
    whole, projected = pl.pallas_call(
        functools.partial(kernel, n_order, n_dp),
        out_shape=(
            jax.ShapeDtypeStruct((per_dp, width, width), F32),
            jax.ShapeDtypeStruct((2, n_dp, per_dp, group, width), BF16),
        ),
        in_specs=[hbm] * 7,
        out_specs=(vmem, any_space),
        scratch_shapes=[
            pltpu.VMEM((1, slot_total), jnp.int32),
            pltpu.SMEM((slots,), jnp.int32),
            pltpu.VMEM((nodes, nodes), BF16),
            pltpu.VMEM((2 * slot_total, samples), BF16),
            pltpu.VMEM((local_images, nodes, samples), BF16),
            pltpu.VMEM((slots, nodes, width), BF16),
            pltpu.VMEM((slots, width, width), BF16),
            pltpu.VMEM((2, slot_total, samples), BF16),
            pltpu.VMEM((slots, nodes, width), BF16),
            pltpu.VMEM((chip_rows * local_images, nodes), F32),
            pltpu.VMEM((n_peers, per_dp, 2, block, nodes), BF16),
            pltpu.VMEM((per_dp, n_order, 2, block, nodes), BF16),
            pltpu.VMEM((per_dp, 2, n_dp, group, width), BF16),
            pltpu.VMEM((per_dp, 2, half, width, width), BF16),
            pltpu.VMEM((per_dp, half, width, width), BF16),
            pltpu.VMEM((per_dp, half, width, width), BF16),
            pltpu.VMEM((per_dp, half, width, width), BF16),
            dma((parts,)),
            dma((6,)),
            dma((n_peers, per_dp)),
            dma((n_peers, per_dp)),
            dma((per_dp,)),
            dma((per_dp,)),
            dma((per_dp, half)),
            dma((per_dp, half)),
            dma((per_dp,)),
        ],
        compiler_params=pltpu.CompilerParams(
            collective_id=0, has_side_effects=True, vmem_limit_bytes=44 * 2**20
        ),
        cost_estimate=pl.CostEstimate(
            flops=5_000_000_000, bytes_accessed=14_000_000, transcendentals=0
        ),
    )(
        *map(
            in_hbm,
            (
                images, radial_interp, assignment.reshape(1, -1), base, counts,
                radial_basis, eigenbasis,
            ),
        )
    )
    projected = projected.reshape(2, slots, group, width)
    return pl.pallas_call(
        finish,
        out_shape=(
            jax.ShapeDtypeStruct((per_dp, 2 * width * width), F32),
            jax.ShapeDtypeStruct(projected.shape, BF16),
        ),
        in_specs=[vmem, any_space],
        out_specs=(vmem, any_space),
        scratch_shapes=[pltpu.VMEM((2 * width * per_dp, width), F32), dma((2, 4))],
        compiler_params=pltpu.CompilerParams(vmem_limit_bytes=16 * 2**20),
        cost_estimate=pl.CostEstimate(
            flops=1_000_000, bytes_accessed=10_000_000, transcendentals=0
        ),
    )(whole, projected)


def solution(mesh):
    placed = (
        P(("dp", "order"), None, None),
        P(),
        P(),
        P("order"),
        P("order", None, None),
        P("order", None, None),
    )
    return jax.shard_map(
        functools.partial(body, mesh.shape["order"], mesh.shape["dp"]),
        mesh=mesh,
        in_specs=placed,
        out_specs=(P(("order", "dp"), None), P(None, "order", "dp", None)),
        check_vma=False,
    )
```

```python
import functools
import math

import jax
import jax.numpy as jnp
import ml_dtypes
import numpy as np
from jax import lax
from jax.experimental import pallas as pl
from jax.experimental.pallas import tpu as pltpu
from jax.sharding import PartitionSpec as P

MESH = pl.DeviceIdType.MESH
BF16 = jnp.bfloat16
F32 = jnp.float32
CORES = 2


def base_table(orders, samples):
    angle = (np.arange(orders)[:, None] * np.arange(samples)[None, :]) % samples
    theta = angle.astype(np.float32) * np.float32(2.0 * math.pi / samples)
    rows = np.concatenate([np.cos(theta), -np.sin(theta)], 0) / np.sqrt(np.float32(samples))
    return rows.astype(ml_dtypes.bfloat16)


def kernel(
    n_order, n_dp, images_hbm, interp_hbm, assignment_hbm, base_hbm, counts_hbm, basis_hbm, eigen_hbm,
    cov_out, proj_out,
    assignment, counts, interp, base, images, basis, eigen, table, kept, wide, send, recv, proj, cov_own, cov_y, cov_z, cov_got,
    coefs, image_sem, weight_sem, spec_send, spec_recv, y_send, y_recv, z_send, z_recv, proj_sem,
):
    local_images, nodes, samples = images.shape
    slots = basis.shape[0]
    chips, half, per_dp = n_order // CORES, n_dp // 2, slots // n_dp
    chip_rows = CORES * slots * 2
    block = n_dp * local_images
    me, my_dp = lax.axis_index("order"), lax.axis_index("dp")
    my_chip, my_core = me // CORES, me % CORES
    my_z, my_y = my_dp // 2, my_dp % 2

    def order_of(dx, dc):
        return lax.rem(my_chip + dx, chips) * CORES + lax.rem(my_core + dc, CORES)

    peers = [(dx, dc) for dx in range(1, chips) for dc in range(CORES)] + [(0, 1)]
    y_peer = my_z * 2 + (1 - my_y)

    def z_peer(q):
        return lax.rem(my_z + q, half)

    barrier = pltpu.get_barrier_semaphore()
    for dx, dc in peers:
        pl.semaphore_signal(barrier, 1, device_id={"order": order_of(dx, dc)}, device_id_type=MESH)
    pl.semaphore_signal(barrier, 1, device_id={"dp": y_peer}, device_id_type=MESH)
    for q in range(1, half):
        pl.semaphore_signal(
            barrier, 1, device_id={"dp": z_peer(q) * 2 + my_y}, device_id_type=MESH
        )

    parts = image_sem.shape[0]
    per_part = local_images // parts
    image_copies = [
        pltpu.make_async_copy(
            images_hbm.at[pl.ds(n * per_part, per_part)],
            images.at[pl.ds(n * per_part, per_part)],
            image_sem.at[n],
        )
        for n in range(parts)
    ]
    base_copy = pltpu.make_async_copy(base_hbm, base, weight_sem.at[2])
    interp_copy = pltpu.make_async_copy(interp_hbm, interp, weight_sem.at[3])
    assignment_copy = pltpu.make_async_copy(assignment_hbm, assignment, weight_sem.at[4])
    counts_copy = pltpu.make_async_copy(counts_hbm, counts, weight_sem.at[5])
    assignment_copy.start()
    counts_copy.start()
    base_copy.start()
    for copy in image_copies:
        copy.start()
    interp_copy.start()
    basis_copy = pltpu.make_async_copy(basis_hbm, basis, weight_sem.at[0])
    eigen_copy = pltpu.make_async_copy(eigen_hbm, eigen, weight_sem.at[1])
    basis_copy.start()
    eigen_copy.start()

    total = n_order * slots
    row = lax.broadcasted_iota(jnp.int32, (total, total), 0)
    lane = lax.broadcasted_iota(jnp.int32, (total, total), 1)
    step = n_dp * CORES
    chip, chunk = lane // (step * per_dp), (lane // step) % per_dp
    core, dp_owner = (lane // n_dp) % CORES, lane % n_dp
    to_row = row == (chip * CORES + core) * slots + dp_owner * per_dp + chunk
    assignment_copy.wait()
    is_order = row == assignment[...]
    pick = jnp.dot(
        is_order.astype(F32).astype(BF16),
        to_row.astype(F32).astype(BF16),
        preferred_element_type=F32,
    ).astype(BF16)
    base_copy.wait()
    for p in range(2):
        table[p] = lax.dot_general(
            pick, base[pl.ds(p * total, total), :],
            (((0,), (0,)), ((), ())), preferred_element_type=F32,
        ).astype(BF16)

    def transform(dx, k0, k1, first):
        at = lax.rem(my_chip + dx, chips) * (step * per_dp) + k0 * step
        count = (k1 - k0) * step
        rows = table[:, pl.ds(pl.multiple_of(at, step), count), :].reshape(2 * count, samples)
        for n in range(parts):
            if first:
                image_copies[n].wait()

            @pl.loop(0, per_part // 2)
            def _(h):
                i = n * per_part + h * 2
                pair = images[pl.ds(i, 2)].reshape(2 * nodes, samples)
                got = lax.dot_general(
                    rows, pair,
                    (((1,), (1,)), ((), ())), preferred_element_type=F32,
                )
                wide[pl.ds(i, 2 * count, stride=local_images), :] = got[:, :nodes]
                wide[pl.ds(i + 1, 2 * count, stride=local_images), :] = got[:, nodes:]

    def spec_copy(k, t):
        dx, dc = peers[t]
        return pltpu.make_async_remote_copy(
            src_ref=send.at[t, k],
            dst_ref=recv.at[k, me],
            send_sem=spec_send.at[t, k],
            recv_sem=spec_recv.at[t, k],
            device_id={"order": order_of(dx, dc)},
            device_id_type=MESH,
        )

    def narrowed(dc, k, k0, k1, p):
        core = lax.rem(my_core + dc, CORES)
        at = pl.multiple_of(((p * (k1 - k0) + k - k0) * CORES + core) * block, block)
        return wide[pl.ds(at, block), :].astype(BF16)

    far = len(peers) - 1
    cuts = sorted({0, 1, min(3, per_dp), per_dp})
    groups = list(zip(cuts[:-1], cuts[1:]))
    for dx in range(1, chips):
        for k0, k1 in groups:
            transform(dx, k0, k1, dx == 1 and k0 == 0)
            if dx == 1 and k0 == 0:
                pl.semaphore_wait(barrier, len(peers) + half)
            for k in range(k0, k1):
                for dc in range(CORES):
                    t = (dx - 1) * CORES + dc
                    for p in range(2):
                        send[t, k, p] = narrowed(dc, k, k0, k1, p)
                    spec_copy(k, t).start()
    transform(0, 0, per_dp, chips == 1)
    for k in range(per_dp):
        for p in range(2):
            send[far, k, p] = narrowed(1, k, 0, per_dp, p)
        spec_copy(k, far).start()
    for k in range(per_dp):
        for p in range(2):
            recv[k, me, p] = narrowed(0, k, 0, per_dp, p)

    basis_copy.wait()
    interp_copy.wait()
    counts_copy.wait()
    column = lax.broadcasted_iota(jnp.int32, (1, kept.shape[2]), 1)

    @pl.loop(0, slots)
    def _(j):
        folded = jnp.dot(interp[...], basis[j], preferred_element_type=F32)
        kept[j] = jnp.where(column < counts[j], folded, 0.0).astype(BF16)

    eigen_copy.wait()
    scale = 1.0 / (local_images * n_order * n_dp)

    def y_copy(k):
        return pltpu.make_async_remote_copy(
            src_ref=cov_own.at[k, 1 - my_y],
            dst_ref=cov_y.at[k],
            send_sem=y_send.at[k],
            recv_sem=y_recv.at[k],
            device_id={"dp": y_peer},
            device_id_type=MESH,
        )

    def z_copy(k, q):
        return pltpu.make_async_remote_copy(
            src_ref=cov_z.at[k, z_peer(q)],
            dst_ref=cov_got.at[k, q],
            send_sem=z_send.at[k, q],
            recv_sem=z_recv.at[k, q],
            device_id={"dp": z_peer(q) * 2 + my_y},
            device_id_type=MESH,
        )

    def proj_copy(k):
        return pltpu.make_async_copy(proj.at[k], proj_out.at[:, :, k], proj_sem.at[k])

    side = n_order * local_images
    batch = 4 if half % 4 == 0 else 1

    def cov_work(k, y):
        @pl.loop(0, half // batch)
        def _(h):
            owners = [(h * batch + n) * 2 + y for n in range(batch)]
            for d in owners:
                at = pl.multiple_of(d * local_images, local_images)
                both = jnp.concatenate(
                    [
                        recv[k, :, p, pl.ds(at, local_images), :].reshape(side, nodes)
                        for p in range(2)
                    ],
                    0,
                )
                coefs[d] = jnp.dot(
                    both, kept[d * per_dp + k], preferred_element_type=F32
                ).astype(BF16)
            for n, d in enumerate(owners):
                coef = coefs[d]
                real, imag = coef[:side], coef[side:]
                mixed = jnp.concatenate([real - imag, real + imag], 0)
                cov = lax.dot_general(
                    coef, mixed, (((0,), (0,)), ((), ())), preferred_element_type=F32
                )
                cov_own[k, y, h * batch + n] = (cov * scale).astype(BF16)

    def proj_work(k):
        @pl.loop(0, n_dp // batch)
        def _(h):
            for n in range(batch):
                d = h * batch + n
                out = jnp.dot(
                    coefs[d], eigen[d * per_dp + k], preferred_element_type=F32
                ).astype(BF16)
                proj[k, 0, d] = out[:side]
                proj[k, 1, d] = out[side:]

    def reduce_y(k):
        y_copy(k).wait_recv()
        cov_z[k] = (cov_own[k, my_y].astype(F32) + cov_y[k].astype(F32)).astype(BF16)
        for q in range(1, half):
            z_copy(k, q).start()

    def reduce_z(k):
        whole = cov_z[k, my_z].astype(F32)
        for q in range(1, half):
            z_copy(k, q).wait_recv()
            whole = whole + cov_got[k, q].astype(F32)
        cov_out[k] = whole

    for k in range(per_dp):
        for t in range(len(peers)):
            spec_copy(k, t).wait_recv()
        cov_work(k, 1 - my_y)
        y_copy(k).start()
        cov_work(k, my_y)
        if k >= 1:
            reduce_y(k - 1)
        proj_work(k)
        proj_copy(k).start()
        if k >= 2:
            reduce_z(k - 2)
    reduce_y(per_dp - 1)
    for k in range(max(0, per_dp - 2), per_dp):
        reduce_z(k)
    for k in range(per_dp):
        for t in range(len(peers)):
            spec_copy(k, t).wait_send()
        y_copy(k).wait_send()
        for q in range(1, half):
            z_copy(k, q).wait_send()
        proj_copy(k).wait()


def finish(whole, proj, cov_out, proj_out, rows, sems):
    parts = [(p, z) for p in range(2) for z in range(sems.shape[1])]
    size = proj.shape[1] // sems.shape[1]
    copies = [
        pltpu.make_async_copy(
            proj.at[p, pl.ds(z * size, size)], proj_out.at[p, pl.ds(z * size, size)], sems.at[p, z]
        )
        for p, z in parts
    ]
    for copy in copies:
        copy.start()
    slots, width, _ = whole.shape
    for k in range(slots):
        one = whole[k]
        flipped = one.T
        rows[pl.ds(k, width, stride=slots), :] = (one + flipped) * 0.5
        rows[pl.ds(width * slots + k, width, stride=slots), :] = (one - flipped) * 0.5
    for r in range(2 * width):
        cov_out[:, pl.ds(r * width, width)] = rows[pl.ds(r * slots, slots), :]
    for copy in copies:
        copy.wait()


def body(n_order, n_dp, images, radial_interp, assignment, counts, radial_basis, eigenbasis):
    local_images, nodes, samples = images.shape
    slot_total = assignment.shape[0]
    slots, _, width = radial_basis.shape
    per_dp, half, chips = slots // n_dp, n_dp // 2, n_order // CORES
    base = jnp.asarray(base_table(slot_total, samples))
    block = n_dp * local_images
    n_peers = n_order - 1
    chip_rows = CORES * slots * 2
    parts = 4
    in_hbm = functools.partial(pltpu.with_memory_space_constraint, memory_space=pltpu.HBM)
    vmem = pl.BlockSpec(memory_space=pltpu.VMEM)
    any_space = pl.BlockSpec(memory_space=pl.ANY)
    hbm = pl.BlockSpec(memory_space=pltpu.HBM)
    dma = pltpu.SemaphoreType.DMA
    group = n_order * local_images
    whole, projected = pl.pallas_call(
        functools.partial(kernel, n_order, n_dp),
        out_shape=(
            jax.ShapeDtypeStruct((per_dp, width, width), F32),
            jax.ShapeDtypeStruct((2, n_dp, per_dp, group, width), BF16),
        ),
        in_specs=[hbm] * 7,
        out_specs=(vmem, any_space),
        scratch_shapes=[
            pltpu.VMEM((1, slot_total), jnp.int32),
            pltpu.SMEM((slots,), jnp.int32),
            pltpu.VMEM((nodes, nodes), BF16),
            pltpu.VMEM((2 * slot_total, samples), BF16),
            pltpu.VMEM((local_images, nodes, samples), BF16),
            pltpu.VMEM((slots, nodes, width), BF16),
            pltpu.VMEM((slots, width, width), BF16),
            pltpu.VMEM((2, slot_total, samples), BF16),
            pltpu.VMEM((slots, nodes, width), BF16),
            pltpu.VMEM((chip_rows * local_images, nodes), F32),
            pltpu.VMEM((n_peers, per_dp, 2, block, nodes), BF16),
            pltpu.VMEM((per_dp, n_order, 2, block, nodes), BF16),
            pltpu.VMEM((per_dp, 2, n_dp, group, width), BF16),
            pltpu.VMEM((per_dp, 2, half, width, width), BF16),
            pltpu.VMEM((per_dp, half, width, width), BF16),
            pltpu.VMEM((per_dp, half, width, width), BF16),
            pltpu.VMEM((per_dp, half, width, width), BF16),
            pltpu.VMEM((n_dp, 2 * group, width), BF16),
            dma((parts,)),
            dma((6,)),
            dma((n_peers, per_dp)),
            dma((n_peers, per_dp)),
            dma((per_dp,)),
            dma((per_dp,)),
            dma((per_dp, half)),
            dma((per_dp, half)),
            dma((per_dp,)),
        ],
        compiler_params=pltpu.CompilerParams(
            collective_id=0, has_side_effects=True, vmem_limit_bytes=44 * 2**20
        ),
        cost_estimate=pl.CostEstimate(
            flops=5_000_000_000, bytes_accessed=14_000_000, transcendentals=0
        ),
    )(
        *map(
            in_hbm,
            (
                images, radial_interp, assignment.reshape(1, -1), base, counts,
                radial_basis, eigenbasis,
            ),
        )
    )
    projected = projected.reshape(2, slots, group, width)
    return pl.pallas_call(
        finish,
        out_shape=(
            jax.ShapeDtypeStruct((per_dp, 2 * width * width), F32),
            jax.ShapeDtypeStruct(projected.shape, BF16),
        ),
        in_specs=[vmem, any_space],
        out_specs=(vmem, any_space),
        scratch_shapes=[pltpu.VMEM((2 * width * per_dp, width), F32), dma((2, 4))],
        compiler_params=pltpu.CompilerParams(vmem_limit_bytes=16 * 2**20),
        cost_estimate=pl.CostEstimate(
            flops=1_000_000, bytes_accessed=10_000_000, transcendentals=0
        ),
    )(whole, projected)


def solution(mesh):
    placed = (
        P(("dp", "order"), None, None),
        P(),
        P(),
        P("order"),
        P("order", None, None),
        P("order", None, None),
    )
    return jax.shard_map(
        functools.partial(body, mesh.shape["order"], mesh.shape["dp"]),
        mesh=mesh,
        in_specs=placed,
        out_specs=(P(("order", "dp"), None), P(None, "order", "dp", None)),
        check_vma=False,
    )
```

```python
import functools
import math

import jax
import jax.numpy as jnp
import ml_dtypes
import numpy as np
from jax import lax
from jax.experimental import pallas as pl
from jax.experimental.pallas import tpu as pltpu
from jax.sharding import PartitionSpec as P

MESH = pl.DeviceIdType.MESH
BF16 = jnp.bfloat16
F32 = jnp.float32
CORES = 2


def base_table(orders, samples):
    angle = (np.arange(orders)[:, None] * np.arange(samples)[None, :]) % samples
    theta = angle.astype(np.float32) * np.float32(2.0 * math.pi / samples)
    rows = np.concatenate([np.cos(theta), -np.sin(theta)], 0) / np.sqrt(np.float32(samples))
    return rows.astype(ml_dtypes.bfloat16)


def kernel(
    n_order, n_dp, images_hbm, interp_hbm, assignment_hbm, base_hbm, counts_hbm, basis_hbm, eigen_hbm,
    cov_out, proj_out,
    assignment, counts, interp, base, images, basis, eigen, table, kept, wide, send, recv, proj, cov_own, cov_y, cov_z, cov_got,
    coefs, image_sem, weight_sem, spec_send, spec_recv, y_send, y_recv, z_send, z_recv, proj_sem,
):
    local_images, nodes, samples = images.shape
    slots = basis.shape[0]
    chips, half, per_dp = n_order // CORES, n_dp // 2, slots // n_dp
    chip_rows = CORES * slots * 2
    block = n_dp * local_images
    me, my_dp = lax.axis_index("order"), lax.axis_index("dp")
    my_chip, my_core = me // CORES, me % CORES
    my_z, my_y = my_dp // 2, my_dp % 2

    def order_of(dx, dc):
        return lax.rem(my_chip + dx, chips) * CORES + lax.rem(my_core + dc, CORES)

    peers = [(dx, dc) for dx in range(1, chips) for dc in range(CORES)] + [(0, 1)]
    y_peer = my_z * 2 + (1 - my_y)

    def z_peer(q):
        return lax.rem(my_z + q, half)

    barrier = pltpu.get_barrier_semaphore()
    for dx, dc in peers:
        pl.semaphore_signal(barrier, 1, device_id={"order": order_of(dx, dc)}, device_id_type=MESH)
    pl.semaphore_signal(barrier, 1, device_id={"dp": y_peer}, device_id_type=MESH)
    for q in range(1, half):
        pl.semaphore_signal(
            barrier, 1, device_id={"dp": z_peer(q) * 2 + my_y}, device_id_type=MESH
        )

    parts = image_sem.shape[0]
    per_part = local_images // parts
    image_copies = [
        pltpu.make_async_copy(
            images_hbm.at[pl.ds(n * per_part, per_part)],
            images.at[pl.ds(n * per_part, per_part)],
            image_sem.at[n],
        )
        for n in range(parts)
    ]
    base_copy = pltpu.make_async_copy(base_hbm, base, weight_sem.at[2])
    interp_copy = pltpu.make_async_copy(interp_hbm, interp, weight_sem.at[3])
    assignment_copy = pltpu.make_async_copy(assignment_hbm, assignment, weight_sem.at[4])
    counts_copy = pltpu.make_async_copy(counts_hbm, counts, weight_sem.at[5])
    assignment_copy.start()
    counts_copy.start()
    base_copy.start()
    for copy in image_copies:
        copy.start()
    interp_copy.start()
    basis_copy = pltpu.make_async_copy(basis_hbm, basis, weight_sem.at[0])
    eigen_copy = pltpu.make_async_copy(eigen_hbm, eigen, weight_sem.at[1])
    basis_copy.start()
    eigen_copy.start()

    total = n_order * slots
    row = lax.broadcasted_iota(jnp.int32, (total, total), 0)
    lane = lax.broadcasted_iota(jnp.int32, (total, total), 1)
    step = n_dp * CORES
    chip, chunk = lane // (step * per_dp), (lane // step) % per_dp
    core, dp_owner = (lane // n_dp) % CORES, lane % n_dp
    to_row = row == (chip * CORES + core) * slots + dp_owner * per_dp + chunk
    assignment_copy.wait()
    is_order = row == assignment[...]
    pick = jnp.dot(
        is_order.astype(F32).astype(BF16),
        to_row.astype(F32).astype(BF16),
        preferred_element_type=F32,
    ).astype(BF16)
    base_copy.wait()
    for p in range(2):
        table[p] = lax.dot_general(
            pick, base[pl.ds(p * total, total), :],
            (((0,), (0,)), ((), ())), preferred_element_type=F32,
        ).astype(BF16)

    def transform(dx, k0, k1, first):
        at = lax.rem(my_chip + dx, chips) * (step * per_dp) + k0 * step
        count = (k1 - k0) * step
        rows = table[:, pl.ds(pl.multiple_of(at, step), count), :].reshape(2 * count, samples)
        for n in range(parts):
            if first:
                image_copies[n].wait()

            @pl.loop(0, per_part // 2)
            def _(h):
                i = n * per_part + h * 2
                pair = images[pl.ds(i, 2)].reshape(2 * nodes, samples)
                got = lax.dot_general(
                    rows, pair,
                    (((1,), (1,)), ((), ())), preferred_element_type=F32,
                )
                wide[pl.ds(i, 2 * count, stride=local_images), :] = got[:, :nodes]
                wide[pl.ds(i + 1, 2 * count, stride=local_images), :] = got[:, nodes:]

    def spec_copy(k, t):
        dx, dc = peers[t]
        return pltpu.make_async_remote_copy(
            src_ref=send.at[t, k],
            dst_ref=recv.at[k, me],
            send_sem=spec_send.at[t, k],
            recv_sem=spec_recv.at[t, k],
            device_id={"order": order_of(dx, dc)},
            device_id_type=MESH,
        )

    def narrowed(dc, k, k0, k1, p):
        core = lax.rem(my_core + dc, CORES)
        at = pl.multiple_of(((p * (k1 - k0) + k - k0) * CORES + core) * block, block)
        return wide[pl.ds(at, block), :].astype(BF16)

    far = len(peers) - 1
    cuts = sorted({0, 1, min(3, per_dp), per_dp})
    groups = list(zip(cuts[:-1], cuts[1:]))
    for dx in range(1, chips):
        for k0, k1 in groups:
            transform(dx, k0, k1, dx == 1 and k0 == 0)
            if dx == 1 and k0 == 0:
                pl.semaphore_wait(barrier, len(peers) + half)
            for k in range(k0, k1):
                for dc in range(CORES):
                    t = (dx - 1) * CORES + dc
                    for p in range(2):
                        send[t, k, p] = narrowed(dc, k, k0, k1, p)
                    spec_copy(k, t).start()
    transform(0, 0, per_dp, chips == 1)
    for k in range(per_dp):
        for p in range(2):
            send[far, k, p] = narrowed(1, k, 0, per_dp, p)
        spec_copy(k, far).start()
    for k in range(per_dp):
        for p in range(2):
            recv[k, me, p] = narrowed(0, k, 0, per_dp, p)

    basis_copy.wait()
    interp_copy.wait()
    counts_copy.wait()
    column = lax.broadcasted_iota(jnp.int32, (1, kept.shape[2]), 1)

    @pl.loop(0, slots)
    def _(j):
        folded = jnp.dot(interp[...], basis[j], preferred_element_type=F32)
        kept[j] = jnp.where(column < counts[j], folded, 0.0).astype(BF16)

    eigen_copy.wait()
    scale = 1.0 / (local_images * n_order * n_dp)

    def y_copy(k):
        return pltpu.make_async_remote_copy(
            src_ref=cov_own.at[k, 1 - my_y],
            dst_ref=cov_y.at[k],
            send_sem=y_send.at[k],
            recv_sem=y_recv.at[k],
            device_id={"dp": y_peer},
            device_id_type=MESH,
        )

    def z_copy(k, q):
        return pltpu.make_async_remote_copy(
            src_ref=cov_z.at[k, z_peer(q)],
            dst_ref=cov_got.at[k, q],
            send_sem=z_send.at[k, q],
            recv_sem=z_recv.at[k, q],
            device_id={"dp": z_peer(q) * 2 + my_y},
            device_id_type=MESH,
        )

    def proj_copy(k):
        return pltpu.make_async_copy(proj.at[k], proj_out.at[:, :, k], proj_sem.at[k])

    side = n_order * local_images
    batch = 4 if half % 4 == 0 else 1

    def cov_work(k, y):
        @pl.loop(0, half // batch)
        def _(h):
            owners = [(h * batch + n) * 2 + y for n in range(batch)]
            for d in owners:
                at = pl.multiple_of(d * local_images, local_images)
                both = jnp.concatenate(
                    [
                        recv[k, :, p, pl.ds(at, local_images), :].reshape(side, nodes)
                        for p in range(2)
                    ],
                    0,
                )
                coefs[d] = jnp.dot(
                    both, kept[d * per_dp + k], preferred_element_type=F32
                ).astype(BF16)
            for n, d in enumerate(owners):
                coef = coefs[d]
                real, imag = coef[:side], coef[side:]
                mixed = jnp.concatenate([real - imag, real + imag], 0)
                cov = lax.dot_general(
                    coef, mixed, (((0,), (0,)), ((), ())), preferred_element_type=F32
                )
                cov_own[k, y, h * batch + n] = (cov * scale).astype(BF16)

    def proj_work(k):
        @pl.loop(0, n_dp // batch)
        def _(h):
            for n in range(batch):
                d = h * batch + n
                out = jnp.dot(
                    coefs[d], eigen[d * per_dp + k], preferred_element_type=F32
                ).astype(BF16)
                proj[k, 0, d] = out[:side]
                proj[k, 1, d] = out[side:]

    def reduce_y(k):
        y_copy(k).wait_recv()
        cov_z[k] = (cov_own[k, my_y].astype(F32) + cov_y[k].astype(F32)).astype(BF16)
        for q in range(1, half):
            z_copy(k, q).start()

    def reduce_z(k):
        whole = cov_z[k, my_z].astype(F32)
        for q in range(1, half):
            z_copy(k, q).wait_recv()
            whole = whole + cov_got[k, q].astype(F32)
        cov_out[k] = whole

    for k in range(per_dp):
        for t in range(len(peers)):
            spec_copy(k, t).wait_recv()
        cov_work(k, 1 - my_y)
        y_copy(k).start()
        cov_work(k, my_y)
        if k >= 1:
            reduce_y(k - 1)
        proj_work(k)
        proj_copy(k).start()
        if k >= 2:
            reduce_z(k - 2)
    reduce_y(per_dp - 1)
    for k in range(max(0, per_dp - 2), per_dp):
        reduce_z(k)
    for k in range(per_dp):
        for t in range(len(peers)):
            spec_copy(k, t).wait_send()
        y_copy(k).wait_send()
        for q in range(1, half):
            z_copy(k, q).wait_send()
        proj_copy(k).wait()


def finish(whole, proj, cov_out, proj_out, rows, cov, sems, cov_sems):
    parts = [(p, z) for p in range(2) for z in range(sems.shape[1])]
    size = proj.shape[1] // sems.shape[1]
    copies = [
        pltpu.make_async_copy(
            proj.at[p, pl.ds(z * size, size)], proj_out.at[p, pl.ds(z * size, size)], sems.at[p, z]
        )
        for p, z in parts
    ]
    for copy in copies:
        copy.start()
    slots, width, _ = whole.shape
    pitch = rows.shape[0] // width
    area = width * width
    for p in range(2):
        for k in range(slots):
            one = whole[k]
            flipped = one.T
            rows[pl.ds(k, width, stride=pitch), :] = (
                one - flipped if p else one + flipped
            ) * 0.5
        for r in range(width):
            cov[:, pl.ds(p * area + r * width, width)] = rows[pl.ds(r * pitch, slots), :]
        copy = pltpu.make_async_copy(
            cov.at[:, pl.ds(p * area, area)], cov_out.at[:, pl.ds(p * area, area)], cov_sems.at[p]
        )
        copy.start()
        copies.append(copy)
    for copy in copies:
        copy.wait()


def body(n_order, n_dp, images, radial_interp, assignment, counts, radial_basis, eigenbasis):
    local_images, nodes, samples = images.shape
    slot_total = assignment.shape[0]
    slots, _, width = radial_basis.shape
    per_dp, half, chips = slots // n_dp, n_dp // 2, n_order // CORES
    base = jnp.asarray(base_table(slot_total, samples))
    block = n_dp * local_images
    n_peers = n_order - 1
    chip_rows = CORES * slots * 2
    parts = 4
    in_hbm = functools.partial(pltpu.with_memory_space_constraint, memory_space=pltpu.HBM)
    vmem = pl.BlockSpec(memory_space=pltpu.VMEM)
    any_space = pl.BlockSpec(memory_space=pl.ANY)
    hbm = pl.BlockSpec(memory_space=pltpu.HBM)
    dma = pltpu.SemaphoreType.DMA
    group = n_order * local_images
    whole, projected = pl.pallas_call(
        functools.partial(kernel, n_order, n_dp),
        out_shape=(
            jax.ShapeDtypeStruct((per_dp, width, width), F32),
            jax.ShapeDtypeStruct((2, n_dp, per_dp, group, width), BF16),
        ),
        in_specs=[hbm] * 7,
        out_specs=(vmem, any_space),
        scratch_shapes=[
            pltpu.VMEM((1, slot_total), jnp.int32),
            pltpu.SMEM((slots,), jnp.int32),
            pltpu.VMEM((nodes, nodes), BF16),
            pltpu.VMEM((2 * slot_total, samples), BF16),
            pltpu.VMEM((local_images, nodes, samples), BF16),
            pltpu.VMEM((slots, nodes, width), BF16),
            pltpu.VMEM((slots, width, width), BF16),
            pltpu.VMEM((2, slot_total, samples), BF16),
            pltpu.VMEM((slots, nodes, width), BF16),
            pltpu.VMEM(((chip_rows + 1) * local_images, nodes), F32),
            pltpu.VMEM((n_peers, per_dp, 2, block, nodes), BF16),
            pltpu.VMEM((per_dp, n_order, 2, block, nodes), BF16),
            pltpu.VMEM((per_dp, 2, n_dp, group, width), BF16),
            pltpu.VMEM((per_dp, 2, half, width, width), BF16),
            pltpu.VMEM((per_dp, half, width, width), BF16),
            pltpu.VMEM((per_dp, half, width, width), BF16),
            pltpu.VMEM((per_dp, half, width, width), BF16),
            pltpu.VMEM((n_dp, 2 * group, width), BF16),
            dma((parts,)),
            dma((6,)),
            dma((n_peers, per_dp)),
            dma((n_peers, per_dp)),
            dma((per_dp,)),
            dma((per_dp,)),
            dma((per_dp, half)),
            dma((per_dp, half)),
            dma((per_dp,)),
        ],
        compiler_params=pltpu.CompilerParams(
            collective_id=0, has_side_effects=True, vmem_limit_bytes=44 * 2**20
        ),
        cost_estimate=pl.CostEstimate(
            flops=5_000_000_000, bytes_accessed=14_000_000, transcendentals=0
        ),
    )(
        *map(
            in_hbm,
            (
                images, radial_interp, assignment.reshape(1, -1), base, counts,
                radial_basis, eigenbasis,
            ),
        )
    )
    projected = projected.reshape(2, slots, group, width)
    return pl.pallas_call(
        finish,
        out_shape=(
            jax.ShapeDtypeStruct((per_dp, 2 * width * width), F32),
            jax.ShapeDtypeStruct(projected.shape, BF16),
        ),
        in_specs=[vmem, any_space],
        out_specs=(any_space, any_space),
        scratch_shapes=[
            pltpu.VMEM((width * (per_dp + 1) + 16, width), F32),
            pltpu.VMEM((per_dp, 2 * width * width), F32),
            dma((2, 4)),
            dma((2,)),
        ],
        compiler_params=pltpu.CompilerParams(vmem_limit_bytes=16 * 2**20),
        cost_estimate=pl.CostEstimate(
            flops=1_000_000, bytes_accessed=10_000_000, transcendentals=0
        ),
    )(whole, projected)


def solution(mesh):
    placed = (
        P(("dp", "order"), None, None),
        P(),
        P(),
        P("order"),
        P("order", None, None),
        P("order", None, None),
    )
    return jax.shard_map(
        functools.partial(body, mesh.shape["order"], mesh.shape["dp"]),
        mesh=mesh,
        in_specs=placed,
        out_specs=(P(("order", "dp"), None), P(None, "order", "dp", None)),
        check_vma=False,
    )
```
